32 devices in a mesh: groups: 2 (over x), gx: 8 (over z, y), gy: 2 (over core).
Axes of the slice: x: 2, y: 2, z: 4, core: 2. Of those that a mesh axis runs over, the one named last changes fastest.
Arguments:
- state: float32 [10, 32, 16, 128], P('groups', 'gx', 'gy'), parts along dimension 0, may hold values from -1.5 to 7, as said below
- closure: float32 [64, 16, 128], P(('groups', 'gx'), 'gy'), parts along dimension 0, may hold values from 0.05 to 0.4
- cotangent: float32 [10, 32, 16, 128], P('groups', 'gx', 'gy'), parts along dimension 0, may hold values from -6 to 6
Outputs:
- grad_state: float32 [10, 32, 16, 128], P('groups', 'gx', 'gy'), parts along dimension 0
- grad_closure: float32 [64, 16, 128], P(('groups', 'gx'), 'gy'), parts along dimension 0
The draws below stay inside these ranges and needn't reach their ends.
There are 2 independent parts, one for each index of `groups`. The reference program is written for one: setup_inputs(seed, part) draws one part's arguments, and reference() takes and returns one part's arrays. A program takes and returns all parts, laid end to end along the dimension named above; each array names one. Nothing has to cross between parts.
Inputs may be any that keep to these rules, and one draw needn't show every extreme that they name: Each cell holds a gas state: rho in 0.5 to 2, pressure 0.4 (E - |m|^2 / (2 rho)) in 0.5 to 2, each velocity component m_d / rho within -0.75 to 0.75.
All inputs are finite; a program needn't handle non-finite values.
Results may differ from the reference program's by a relative error of at most 0.00006.
Values sent between devices are 32-bit elements; how exact they have to be, the bound alone decides.
A program may use at most 128 MiB of HBM per device.

```python
import math
import jax
import jax.numpy as jnp
from jax import lax

NX = 32
NY = 16
NZ = 128


def draw_state(key, part):
    key = jax.random.fold_in(key, 11)
    keys = jax.random.split(key, 3)
    shape = (NX, NY, NZ)
    density = jnp.exp(jax.random.uniform(keys[0], shape, jnp.float32, math.log(0.5), math.log(2.0)))
    velocity = jnp.clip(0.25 * jax.random.normal(keys[1], (3,) + shape, jnp.float32), -0.75, 0.75)
    pressure = jax.random.uniform(keys[2], shape, jnp.float32, 0.5, 2.0)
    momenta = density[None] * velocity
    energy = pressure / 0.4 + 0.5 * density * jnp.sum(velocity * velocity, axis=0)
    return jnp.concatenate([density[None], momenta, energy[None]], axis=0).astype(jnp.float32)


def shard_levels(rng, shape, pieces, least, top_value):
    def one(axis_at, shards_of):
        draws = jax.random.uniform(jax.random.fold_in(jax.random.fold_in(rng, 6), axis_at), (shards_of,), jnp.float32, least / len(pieces), top_value / len(pieces))
        return jnp.repeat(jnp.exp(draws), shape[axis_at] // shards_of).reshape((-1,) + (1,) * (len(shape) - axis_at - 1))

    loudness = one(*pieces[0])
    for cut in pieces[1:]:
        loudness = loudness * one(*cut)
    return loudness


def centred(own_key, dims, width, bound, cuts=(), kind=jnp.bfloat16):
    loudness = shard_levels(own_key, dims, cuts, -0.22, 0.18) if cuts else 1.0
    drawn = jax.random.normal(own_key, dims, jnp.float32) * width * loudness
    return jnp.minimum(jnp.maximum(drawn, -bound), bound).astype(kind)


def setup_inputs(seed: int = 0, part: int = 0) -> dict:
    arg_keys = jax.random.split(jax.random.key(seed), 4)
    own_keys = jax.random.split(jax.random.fold_in(arg_keys[3], part), 4)
    return {
        "state": draw_state(jax.random.fold_in(jax.random.fold_in(arg_keys[3], part), 71), part),
        "closure": jnp.clip(jnp.exp(math.log(0.4) - 2.0794415 * jax.random.uniform(own_keys[1], (NX, NY, NZ), jnp.float32) ** shard_levels(own_keys[1], (NX, NY, NZ), ((0, 8), (1, 2)), -0.2, 0.2)), 0.05, 0.4),
        "cotangent": centred(own_keys[2], (5, NX, NY, NZ), 1.0, 6.0, ((1, 8), (2, 2)), jnp.float32),
    }


WENO_EPS = 1e-06
TIME_STEP = 0.06
SECTION_WEIGHTS = ((0.0, 1.0), (0.75, 0.25), (1.0 / 3.0, 2.0 / 3.0))

def window(block, start, extent, along):
    return lax.slice_in_dim(block, start, start + extent, axis=along)

def split_fluxes(fields, direction):
    density = fields[0]
    energy = fields[4]
    inverse = 1.0 / density
    kinetic = 0.5 * (fields[1] * fields[1] + fields[2] * fields[2] + fields[3] * fields[3]) * inverse
    pressure = 0.4 * (energy - kinetic)
    speed = fields[1 + direction] * inverse
    wave_speed = 1.5 * jnp.sqrt(speed * speed + 1.4 * pressure * inverse)
    fluxes = [fields[1 + direction], fields[1] * speed, fields[2] * speed, fields[3] * speed, (energy + pressure) * speed]
    fluxes[1 + direction] = fluxes[1 + direction] + pressure
    fluxes = jnp.stack(fluxes)
    upwind = 0.5 * (fluxes + wave_speed * fields)
    downwind = 0.5 * (fluxes - wave_speed * fields)
    return (upwind, downwind)

def weno_face(left_two, left_one, centre, right_one, right_two):
    cand_zero = (2.0 * left_two - 7.0 * left_one + 11.0 * centre) / 6.0
    cand_one = (-left_one + 5.0 * centre + 2.0 * right_one) / 6.0
    cand_two = (2.0 * centre + 5.0 * right_one - right_two) / 6.0
    rough_zero = 13.0 / 12.0 * (left_two - 2.0 * left_one + centre) ** 2 + 0.25 * (left_two - 4.0 * left_one + 3.0 * centre) ** 2
    rough_one = 13.0 / 12.0 * (left_one - 2.0 * centre + right_one) ** 2 + 0.25 * (left_one - right_one) ** 2
    rough_two = 13.0 / 12.0 * (centre - 2.0 * right_one + right_two) ** 2 + 0.25 * (3.0 * centre - 4.0 * right_one + right_two) ** 2
    weight_zero = 0.1 / (WENO_EPS + rough_zero) ** 2
    weight_one = 0.6 / (WENO_EPS + rough_one) ** 2
    weight_two = 0.3 / (WENO_EPS + rough_two) ** 2
    return (weight_zero * cand_zero + weight_one * cand_one + weight_two * cand_two) / (weight_zero + weight_one + weight_two)

def axis_rate(upwind, downwind, along, extent):
    faces = extent + 1
    upper = weno_face(window(upwind, 0, faces, along), window(upwind, 1, faces, along), window(upwind, 2, faces, along), window(upwind, 3, faces, along), window(upwind, 4, faces, along))
    lower = weno_face(window(downwind, 5, faces, along), window(downwind, 4, faces, along), window(downwind, 3, faces, along), window(downwind, 2, faces, along), window(downwind, 1, faces, along))
    face_flux = upper + lower
    return window(face_flux, 0, extent, along) - window(face_flux, 1, extent, along)

def cyclic_rate(upwind, downwind, along):
    upper = weno_face(jnp.roll(upwind, 2, axis=along), jnp.roll(upwind, 1, axis=along), upwind, jnp.roll(upwind, -1, axis=along), jnp.roll(upwind, -2, axis=along))
    lower = weno_face(jnp.roll(downwind, -3, axis=along), jnp.roll(downwind, -2, axis=along), jnp.roll(downwind, -1, axis=along), downwind, jnp.roll(downwind, 1, axis=along))
    face_flux = upper + lower
    return jnp.roll(face_flux, 1, axis=along) - face_flux

def tendency(padded, closure):
    wide_x = padded.shape[1] - 6
    wide_y = padded.shape[2] - 6
    along_x = padded[:, :, 3:3 + wide_y, :]
    along_y = padded[:, 3:3 + wide_x, :, :]
    centre = padded[:, 3:3 + wide_x, 3:3 + wide_y, :]
    upwind, downwind = split_fluxes(along_x, 0)
    total = axis_rate(upwind, downwind, 1, wide_x)
    upwind, downwind = split_fluxes(along_y, 1)
    total = total + axis_rate(upwind, downwind, 2, wide_y)
    upwind, downwind = split_fluxes(centre, 2)
    total = total + cyclic_rate(upwind, downwind, 3)
    laplace = window(along_x, 2, wide_x, 1) + window(along_x, 4, wide_x, 1) + (window(along_y, 2, wide_y, 2) + window(along_y, 4, wide_y, 2)) + (jnp.roll(centre, 1, axis=3) + jnp.roll(centre, -1, axis=3)) - 6.0 * centre
    viscous = closure[None] * laplace[1:]
    return jnp.concatenate([total[:1], total[1:] + viscous], axis=0)

def reference(state, closure, cotangent):
    checked = jax.checkpoint(tendency)

    def advance(fields, closure_field):
        current = fields
        for weight_base, weight_section in SECTION_WEIGHTS:
            padded = jnp.pad(current, ((0, 0), (3, 3), (3, 3), (0, 0)), mode='wrap')
            current = weight_base * fields + weight_section * (current + TIME_STEP * checked(padded, closure_field))
        return current
    _, pullback = jax.vjp(advance, state, closure)
    grad_state, grad_closure = pullback(cotangent)
    return (grad_state, grad_closure)
```

```python
import functools
import jax
import jax.numpy as jnp
from jax import lax
from jax.experimental import pallas as pl
from jax.experimental.pallas import tpu as pltpu
from jax.sharding import PartitionSpec as P

WENO_EPS = 1e-06
TIME_STEP = 0.06
SECTION_WEIGHTS = ((0.0, 1.0), (0.75, 0.25), (1.0 / 3.0, 2.0 / 3.0))
HALO = 3
MESH = pl.DeviceIdType.MESH


def inverse_of(value):
    return 1.0 / value


def shifted(value, steps, axis):
    return pltpu.roll(value, (-steps) % value.shape[axis], axis)


def cell_terms(q, direction):
    inverse = inverse_of(q[0])
    squares = q[1] * q[1] + q[2] * q[2] + q[3] * q[3]
    pressure = 0.4 * (q[4] - 0.5 * squares * inverse)
    speed = q[1 + direction] * inverse
    inside = speed * speed + 1.4 * pressure * inverse
    root = lax.rsqrt(inside)
    return inverse, squares, pressure, speed, 1.5 * inside * root, root


def split_fluxes(q, direction):
    _, _, pressure, speed, wave, _ = cell_terms(q, direction)
    flux = [q[1 + direction], q[1] * speed, q[2] * speed, q[3] * speed, (q[4] + pressure) * speed]
    flux[1 + direction] = flux[1 + direction] + pressure
    half = 0.5 * wave
    up, down = [], []
    for c in range(5):
        centre, spread = 0.5 * flux[c], half * q[c]
        up.append(centre + spread)
        down.append(centre - spread)
    return up, down


def split_fluxes_back(q, up, down, direction):
    inverse, squares, pressure, speed, wave, root = cell_terms(q, direction)
    flux = [0.5 * (up[c] + down[c]) for c in range(5)]
    diff = [0.5 * (up[c] - down[c]) for c in range(5)]
    grad = [wave * diff[c] for c in range(5)]
    wave_bar = diff[0] * q[0] + diff[1] * q[1] + diff[2] * q[2] + diff[3] * q[3] + diff[4] * q[4]
    wave_bar = (1.5 * wave_bar) * root
    lift = flux[4] * speed
    ratio_bar = 0.7 * wave_bar
    speed_bar = (
        flux[1] * q[1] + flux[2] * q[2] + flux[3] * q[3]
        + flux[4] * (q[4] + pressure) + wave_bar * speed
    )
    pressure_bar = flux[1 + direction] + lift + ratio_bar * inverse
    inverse_bar = ratio_bar * pressure + speed_bar * q[1 + direction] - (0.2 * pressure_bar) * squares
    slope = 0.4 * pressure_bar
    pull = slope * inverse
    for k in range(1, 4):
        grad[k] = grad[k] + flux[k] * speed - pull * q[k]
    grad[1 + direction] = grad[1 + direction] + flux[0] + speed_bar * inverse
    grad[4] = grad[4] + lift + slope
    grad[0] = grad[0] - inverse_bar * inverse * inverse
    return grad


def rough(bend):
    return WENO_EPS + (13.0 / 12.0) * bend * bend


def weno(centre, d1, d2, s0, s1, s2, m0, m1, m2, sign):
    half = 0.5 * sign
    t0, t1, t2 = d1 + half * s0, d1 + half * s1, d2 - half * s2
    r0, r1, r2 = inverse_of(m0 + t0 * t0), inverse_of(m1 + t1 * t1), inverse_of(m2 + t2 * t2)
    w0, w1, w2 = r0 * r0, 6.0 * (r1 * r1), 3.0 * (r2 * r2)
    scale = inverse_of(w0 + w1 + w2)
    w0, w1, w2 = w0 * scale, w1 * scale, w2 * scale
    e0, e1 = (1.0 / 3.0) * s0, (1.0 / 3.0) * s1
    e2 = 0.5 * s1 - (1.0 / 6.0) * s2
    mean = w0 * e0 + w1 * e1 + w2 * e2
    face = centre + half * d1 + mean
    c0 = w0 * r0 * (mean - e0)
    c1 = w1 * r1 * (mean - e1)
    c2 = w2 * r2 * (mean - e2)
    c0, c1, c2 = c0 + c0, c1 + c1, c2 + c2
    k = 13.0 / 6.0
    p0, p1, p2 = c0 * t0, c1 * t1, c2 * t2
    third = 1.0 / 3.0
    if sign > 0:
        a0 = third * w0 + k * (c0 * s0) + p0
        a1 = third * w1 + 0.5 * w2 + k * (c1 * s1) + p1
        a2 = k * (c2 * s2) - (1.0 / 6.0) * w2 - p2
    else:
        a0 = third * w0 + k * (c0 * s0) - p0
        a1 = third * w1 + 0.5 * w2 + k * (c1 * s1) - p1
        a2 = k * (c2 * s2) - (1.0 / 6.0) * w2 + p2
    g1 = half + 2.0 * (p0 + p1)
    g2 = 2.0 * p2
    return face, (a0, a1, a2, g1, g2)


def ring_weno(f, axis, sign):
    ahead = shifted(f, 1, axis) - f
    behind = shifted(ahead, -1, axis)
    bend = ahead - behind
    m = rough(bend)
    below, above = shifted(bend, -1, axis), shifted(bend, 1, axis)
    if sign > 0:
        return weno(f, behind, ahead, below, bend, above, rough(below), m, rough(above), 1.0)
    return weno(f, ahead, behind, above, bend, below, rough(above), m, rough(below), -1.0)


def ring_weno_back(mu, coef, axis, sign):
    a0, a1, a2, g1, g2 = [k * mu for k in coef]
    if sign > 0:
        bend = shifted(a0, 1, axis) + a1 + shifted(a2, -1, axis)
        ahead = g2 + bend + shifted(g1 - bend, 1, axis)
    else:
        bend = shifted(a0, -1, axis) + a1 + shifted(a2, 1, axis)
        ahead = g1 + bend + shifted(g2 - bend, 1, axis)
    return mu + shifted(ahead, -1, axis) - ahead


def plus(total, term):
    return term if total is None else total + term


def kernel(
    n, state, closure, cotangent, out_state, out_closure,
    q, other, coef_x, coef_y, coef_z, lap, fx, fy, fz, rate,
    lam, weight, total, gx, go, gin, rx_low, rx_high, ro, send, recv,
):
    wide = n + 2 * HALO
    mine = pl.ds(HALO, n)
    count = lax.axis_size("gx")
    me = lax.axis_index("gx")
    right, left = lax.rem(me + 1, count), lax.rem(me + count - 1, count)
    across = 1 - lax.axis_index("gy")
    barrier = pltpu.get_barrier_semaphore()
    for target in ({"gx": left}, {"gx": right}, {"gy": across}):
        pl.semaphore_signal(barrier, inc=1, device_id=target, device_id_type=MESH)

    q[0, :, mine] = state[...]
    pl.semaphore_wait(barrier, 3)

    def three(number, sources, targets):
        made = []
        for k, (source, landing, target) in enumerate(
            zip(sources, targets, ({"gx": left}, {"gx": right}, {"gy": across}))
        ):
            made.append(
                pltpu.make_async_remote_copy(
                    src_ref=source, dst_ref=landing,
                    send_sem=send.at[number, k], recv_sem=recv.at[number, k],
                    device_id=target, device_id_type=MESH,
                )
            )
        return made

    pending = []

    def each(body, length=5):
        def step(i, carry):
            body(i)
            return carry
        lax.fori_loop(0, length, step, 0)

    def ring_y(s, c):
        return jnp.concatenate([q[s, c, mine], other[s, c]], axis=1)

    def forward(s):
        last = s == 2
        copies = three(
            s,
            (q.at[s, :, pl.ds(HALO, HALO)], q.at[s, :, pl.ds(n, HALO)], q.at[s, :, mine]),
            (q.at[s, :, pl.ds(n + HALO, HALO)], q.at[s, :, pl.ds(0, HALO)], other.at[s]),
        )
        for copy in (copies[2], copies[0], copies[1]):
            copy.start()
        pending.extend(copies)

        up, down = split_fluxes([q[s, c, mine] for c in range(5)], 2)
        for c in range(5):
            fz[0, c] = up[c]
            fz[1, c] = down[c]

        def along_z(c):
            face, coef = ring_weno(fz[0, c], 2, 1)
            face_low, coef_low = ring_weno(fz[1, c], 2, -1)
            for k in range(5):
                coef_z[s, c, 0, k] = coef[k]
                coef_z[s, c, 1, k] = coef_low[k]
            if not last:
                face = face + shifted(face_low, 1, 2)
                rate[c] = shifted(face, -1, 2) - face
            own = q[s, c, mine]
            lap[s, c] = shifted(own, -1, 2) + shifted(own, 1, 2) - 6.0 * own

        each(along_z)
        copies[2].wait_recv()
        up, down = split_fluxes([ring_y(s, c) for c in range(5)], 1)
        for c in range(5):
            fy[0, c] = up[c]
            fy[1, c] = down[c]

        def along_y(c):
            face, coef = ring_weno(fy[0, c], 1, 1)
            face_low, coef_low = ring_weno(fy[1, c], 1, -1)
            for k in range(5):
                coef_y[s, c, 0, k] = coef[k]
                coef_y[s, c, 1, k] = coef_low[k]
            if not last:
                face = face + shifted(face_low, 1, 1)
                rate[c] += (shifted(face, -1, 1) - face)[:, :8]
            both = ring_y(s, c)
            lap[s, c] += (shifted(both, -1, 1) + shifted(both, 1, 1))[:, :8]

        each(along_y)
        copies[0].wait_recv()
        copies[1].wait_recv()

        def flux_x(i):
            at = pl.ds(2 * i, 2)
            up, down = split_fluxes([q[s, c, at] for c in range(5)], 0)
            for c in range(5):
                fx[0, c, at] = up[c]
                fx[1, c, at] = down[c]

        each(flux_x, wide // 2)
        weight_base, weight_section = SECTION_WEIGHTS[s]

        def along_x(c):
            faces = [None] * (n + 1)
            for side, sign in ((0, 1), (1, -1)):
                f = [fx[side, c, i] for i in range(wide)]
                d = [f[i + 1] - f[i] for i in range(wide - 1)]
                bend = [None] + [d[i] - d[i - 1] for i in range(1, wide - 1)]
                m = [None] + [rough(b) for b in bend[1:]]
                for face in range(n + 1):
                    if sign > 0:
                        i = face + 2
                        value, coef = weno(
                            f[i], d[i - 1], d[i], bend[i - 1], bend[i], bend[i + 1],
                            m[i - 1], m[i], m[i + 1], 1.0)
                    else:
                        i = face + 3
                        value, coef = weno(
                            f[i], d[i], d[i - 1], bend[i + 1], bend[i], bend[i - 1],
                            m[i + 1], m[i], m[i - 1], -1.0)
                    faces[face] = plus(faces[face], value)
                    for k in range(5):
                        coef_x[s, c, side, k, face] = coef[k]
            on = jnp.where(c > 0, 1.0, 0.0)
            for x in range(n):
                i = x + HALO
                whole = lap[s, c, x] + q[s, c, i - 1] + q[s, c, i + 1]
                whole = whole * on
                lap[s, c, x] = whole
                if not last:
                    speed = rate[c, x] + (faces[x] - faces[x + 1]) + closure[x] * whole
                    q[s + 1, c, i] = (
                        weight_base * q[0, c, i] + weight_section * (q[s, c, i] + TIME_STEP * speed)
                    )

        each(along_x)

    def backward(s):
        weight_base, weight_section = SECTION_WEIGHTS[s]

        def along_x(c):
            on = jnp.where(c > 0, 1.0, 0.0)
            load = []
            for x in range(n):
                here = weight[c, x]
                total[c, x] += weight_base * here
                load.append((TIME_STEP * weight_section) * here)
                lam[c, x] = load[x]
                gin[c, x] = weight_section * here
            mus = [load[0]] + [load[x] - load[x - 1] for x in range(1, n)] + [-load[n - 1]]
            for side, sign in ((0, 1), (1, -1)):
                bend = [None] * wide
                ahead = [None] * wide
                value = [None] * wide
                for face in range(n + 1):
                    mu = mus[face]
                    a0, a1, a2, g1, g2 = [coef_x[s, c, side, k, face] * mu for k in range(5)]
                    i = face + 2 if sign > 0 else face + 3
                    value[i] = mu
                    bend[i] = plus(bend[i], a1)
                    bend[i - sign] = plus(bend[i - sign], a0)
                    bend[i + sign] = plus(bend[i + sign], a2)
                    first, second = (i - 1, i) if sign > 0 else (i, i - 1)
                    ahead[first] = plus(ahead[first], g1)
                    ahead[second] = plus(ahead[second], g2)
                for i in range(wide):
                    if bend[i] is not None:
                        ahead[i] = plus(ahead[i], bend[i])
                        ahead[i - 1] = plus(ahead[i - 1], -bend[i])
                for i in range(wide):
                    if ahead[i] is not None:
                        value[i + 1] = plus(value[i + 1], ahead[i])
                        value[i] = plus(value[i], -ahead[i])
                for i in range(wide):
                    fx[side, c, i] = jnp.zeros_like(mus[0]) if value[i] is None else value[i]
            kappa = [on * closure[x] * load[x] for x in range(n)]
            for i in range(wide):
                x = i - HALO
                term = None
                if 0 <= x - 1 < n:
                    term = plus(term, kappa[x - 1])
                if 0 <= x + 1 < n:
                    term = plus(term, kappa[x + 1])
                if 0 <= x < n:
                    term = plus(term, -6.0 * kappa[x])
                gx[s, c, i] = jnp.zeros_like(mus[0]) if term is None else term

        each(along_x)

        def pull_x(i):
            at = pl.ds(2 * i, 2)
            grad = split_fluxes_back(
                [q[s, c, at] for c in range(5)],
                [fx[0, c, at] for c in range(5)],
                [fx[1, c, at] for c in range(5)], 0)
            for c in range(5):
                gx[s, c, at] += grad[c]

        each(pull_x, wide // 2)
        copies = three(
            HALO + s,
            (gx.at[s, :, pl.ds(0, HALO)], gx.at[s, :, pl.ds(n + HALO, HALO)], go.at[s]),
            (rx_high.at[s], rx_low.at[s], ro.at[s]),
        )
        copies[0].start()
        copies[1].start()

        def along_y(c):
            on = jnp.where(c > 0, 1.0, 0.0)
            own = lam[c]
            ring = jnp.concatenate([own, jnp.zeros_like(own)], axis=1)
            mu = shifted(ring, 1, 1) - ring
            nu = ring - shifted(ring, -1, 1)
            fy[0, c] = ring_weno_back(mu, [coef_y[s, c, 0, k] for k in range(5)], 1, 1)
            fy[1, c] = ring_weno_back(nu, [coef_y[s, c, 1, k] for k in range(5)], 1, -1)
            kappa = own * closure[...] * on
            ring = jnp.concatenate([kappa, jnp.zeros_like(own)], axis=1)
            both = shifted(ring, 1, 1) + shifted(ring, -1, 1)
            gin[c] += both[:, :8] + shifted(kappa, 1, 2) + shifted(kappa, -1, 2)
            go[s, c] = both[:, 8:]

        each(along_y)

        def pull_y(x):
            grad = split_fluxes_back(
                [jnp.concatenate([q[s, c, x + HALO], other[s, c, x]], axis=0) for c in range(5)],
                [fy[0, c, x] for c in range(5)],
                [fy[1, c, x] for c in range(5)], 1)
            for c in range(5):
                gin[c, x] += grad[c][:8]
                go[s, c, x] += grad[c][8:]

        each(pull_y, n)
        copies[2].start()
        pending.extend(copies)

        def along_z(c):
            own = lam[c]
            mu = shifted(own, 1, 2) - own
            nu = own - shifted(own, -1, 2)
            fz[0, c] = ring_weno_back(mu, [coef_z[s, c, 0, k] for k in range(5)], 2, 1)
            fz[1, c] = ring_weno_back(nu, [coef_z[s, c, 1, k] for k in range(5)], 2, -1)

        each(along_z)

        def pull_z(i):
            at = pl.ds(2 * i, 2)
            inner = pl.ds(2 * i + HALO, 2)
            grad = split_fluxes_back(
                [q[s, c, inner] for c in range(5)],
                [fz[0, c, at] for c in range(5)],
                [fz[1, c, at] for c in range(5)], 2)
            for c in range(5):
                gin[c, at] += grad[c] + gx[s, c, inner]

        each(pull_z, n // 2)
        share = lam[1] * lap[s, 1]
        for c in range(2, 5):
            share = share + lam[c] * lap[s, c]
        out_closure[...] = share if s == 2 else out_closure[...] + share
        for copy in copies:
            copy.wait_recv()

        def gather(c):
            weight[c] = gin[c] + ro[s, c]
            weight[c, pl.ds(n - HALO, HALO)] += rx_high[s, c]
            weight[c, pl.ds(0, HALO)] += rx_low[s, c]

        each(gather)

    for s in range(3):
        forward(s)
    weight[...] = cotangent[...]
    total[...] = jnp.zeros_like(total)
    for s in (2, 1, 0):
        backward(s)
    out_state[...] = total[...] + weight[...]
    for copy in pending:
        copy.wait_send()


def local(state, closure, cotangent):
    _, n, rows, lanes = state.shape
    f32 = jnp.float32
    wide = n + 2 * HALO
    plane = (rows, lanes)

    def vmem(*shape):
        return pltpu.VMEM(shape + plane, f32)

    def tall(*shape):
        return pltpu.VMEM(shape + (2 * rows, lanes), f32)

    return pl.pallas_call(
        functools.partial(kernel, n),
        out_shape=(
            jax.ShapeDtypeStruct(state.shape, f32),
            jax.ShapeDtypeStruct(closure.shape, f32),
        ),
        in_specs=[pl.BlockSpec(memory_space=pltpu.VMEM)] * 3,
        out_specs=(pl.BlockSpec(memory_space=pltpu.VMEM),) * 2,
        scratch_shapes=[
            vmem(3, 5, wide), vmem(3, 5, n),
            vmem(3, 5, 2, 5, n + 1), tall(3, 5, 2, 5, n), vmem(3, 5, 2, 5, n),
            vmem(3, 5, n), vmem(2, 5, wide), tall(2, 5, n), vmem(2, 5, n), vmem(5, n),
            vmem(5, n), vmem(5, n), vmem(5, n),
            vmem(3, 5, wide), vmem(3, 5, n), vmem(5, n),
            vmem(3, 5, HALO), vmem(3, 5, HALO), vmem(3, 5, n),
            pltpu.SemaphoreType.DMA((6, 3)), pltpu.SemaphoreType.DMA((6, 3)),
        ],
        compiler_params=pltpu.CompilerParams(
            collective_id=0, has_side_effects=True, vmem_limit_bytes=40 * 1024 * 1024
        ),
    )(state, closure, cotangent)


def solution(mesh):
    placed = (
        P("groups", "gx", "gy", None),
        P(("groups", "gx"), "gy", None),
        P("groups", "gx", "gy", None),
    )
    return jax.shard_map(
        local,
        mesh=mesh,
        in_specs=placed,
        out_specs=(P("groups", "gx", "gy", None), P(("groups", "gx"), "gy", None)),
        check_vma=False,
    )
```

```python
import functools
import jax
import jax.numpy as jnp
from jax import lax
from jax.experimental import pallas as pl
from jax.experimental.pallas import tpu as pltpu
from jax.sharding import PartitionSpec as P

WENO_EPS = 1e-06
TIME_STEP = 0.06
SECTION_WEIGHTS = ((0.0, 1.0), (0.75, 0.25), (1.0 / 3.0, 2.0 / 3.0))
HALO = 3
MESH = pl.DeviceIdType.MESH


def inverse_of(value):
    return 1.0 / value


def shifted(value, steps, axis):
    return pltpu.roll(value, (-steps) % value.shape[axis], axis)


def cell_terms(q, direction):
    inverse = inverse_of(q[0])
    squares = q[1] * q[1] + q[2] * q[2] + q[3] * q[3]
    pressure = 0.4 * (q[4] - 0.5 * squares * inverse)
    speed = q[1 + direction] * inverse
    inside = speed * speed + 1.4 * pressure * inverse
    root = lax.rsqrt(inside)
    return inverse, squares, pressure, speed, 1.5 * inside * root, root


def split_fluxes(q, direction):
    _, _, pressure, speed, wave, _ = cell_terms(q, direction)
    flux = [q[1 + direction], q[1] * speed, q[2] * speed, q[3] * speed, (q[4] + pressure) * speed]
    flux[1 + direction] = flux[1 + direction] + pressure
    half = 0.5 * wave
    up, down = [], []
    for c in range(5):
        centre, spread = 0.5 * flux[c], half * q[c]
        up.append(centre + spread)
        down.append(centre - spread)
    return up, down


def split_fluxes_back(q, up, down, direction):
    inverse, squares, pressure, speed, wave, root = cell_terms(q, direction)
    flux = [0.5 * (up[c] + down[c]) for c in range(5)]
    diff = [0.5 * (up[c] - down[c]) for c in range(5)]
    grad = [wave * diff[c] for c in range(5)]
    wave_bar = diff[0] * q[0] + diff[1] * q[1] + diff[2] * q[2] + diff[3] * q[3] + diff[4] * q[4]
    wave_bar = (1.5 * wave_bar) * root
    lift = flux[4] * speed
    ratio_bar = 0.7 * wave_bar
    speed_bar = (
        flux[1] * q[1] + flux[2] * q[2] + flux[3] * q[3]
        + flux[4] * (q[4] + pressure) + wave_bar * speed
    )
    pressure_bar = flux[1 + direction] + lift + ratio_bar * inverse
    inverse_bar = ratio_bar * pressure + speed_bar * q[1 + direction] - (0.2 * pressure_bar) * squares
    slope = 0.4 * pressure_bar
    pull = slope * inverse
    for k in range(1, 4):
        grad[k] = grad[k] + flux[k] * speed - pull * q[k]
    grad[1 + direction] = grad[1 + direction] + flux[0] + speed_bar * inverse
    grad[4] = grad[4] + lift + slope
    grad[0] = grad[0] - inverse_bar * inverse * inverse
    return grad


def rough(bend):
    return WENO_EPS + (13.0 / 12.0) * bend * bend


def weno(centre, d1, d2, s0, s1, s2, m0, m1, m2, sign):
    h0, h1, h2 = 0.5 * s0, 0.5 * s1, 0.5 * s2
    if sign > 0:
        t0, t1, t2 = h0 + d1, h1 + d1, h2 - d2
        base = centre + 0.5 * d1
    else:
        t0, t1, t2 = h0 - d1, h1 - d1, h2 + d2
        base = centre - 0.5 * d1
    r0, r1, r2 = inverse_of(m0 + t0 * t0), inverse_of(m1 + t1 * t1), inverse_of(m2 + t2 * t2)
    w0, w1, w2 = r0 * r0, 6.0 * (r1 * r1), 3.0 * (r2 * r2)
    scale = inverse_of(w0 + w1 + w2)
    w0, w1, w2 = w0 * scale, w1 * scale, w2 * scale
    third, sixth = 1.0 / 3.0, 1.0 / 6.0
    e0, e1, e2 = third * s0, third * s1, h1 - sixth * s2
    mean = w0 * e0 + w1 * e1 + w2 * e2
    c0, c1, c2 = w0 * r0 * (mean - e0), w1 * r1 * (mean - e1), w2 * r2 * (mean - e2)
    k = 13.0 / 3.0
    p0, p1, p2 = 2.0 * (c0 * t0), 2.0 * (c1 * t1), 2.0 * (c2 * t2)
    a0 = third * w0 + k * (c0 * s0) + p0
    a1 = third * w1 + 0.5 * w2 + k * (c1 * s1) + p1
    a2 = k * (c2 * s2) - sixth * w2 + p2
    j1 = a1 - 2.0 * a0 - (0.5 + 2.0 * (p0 + p1))
    j3 = a1 - 2.0 * (a2 + p2)
    j2 = 1.0 - (a0 + a2) - (j1 + j3)
    return base + mean, (a0, j1, j2, j3, a2)


def weno_of(v0, v1, v2, v3, v4):
    d0, d1, d2, d3 = v1 - v0, v2 - v1, v3 - v2, v4 - v3
    s0, s1, s2 = d1 - d0, d2 - d1, d3 - d2
    return weno(v2, d1, d2, s0, s1, s2, rough(s0), rough(s1), rough(s2), 1)


def ring_weno(f, axis, sign):
    v = [shifted(f, k, axis) if k else f for k in (-2, -1, 0, 1, 2)]
    return weno_of(*v[::sign])


def ring_weno_back(mu, coef, axis, sign):
    total = coef[2] * mu
    for k in (0, 1, 3, 4):
        total = total + shifted(coef[k] * mu, sign * (2 - k), axis)
    return total


def plus(total, term):
    return term if total is None else total + term


def kernel(
    n, state, closure_in, cotangent, out_state, out_closure, closure,
    q, other, coef_x, coef_y, coef_z, lap, fx, fy, fz, rate,
    lam, weight, total, gx, go, gin, rx_low, rx_high, ro, send, recv,
    home, home_closure, grad_closure, route_send, route_recv,
):
    wide = n + 2 * HALO
    mine = pl.ds(HALO, n)
    count = lax.axis_size("gx")
    me = lax.axis_index("gx")
    folded = count == 8
    if folded:
        block = lax.rem(me // 2 + (me % 2) * (count - 1 - 2 * (me // 2)) + 2, count)
    else:
        block = me

    def around(b):
        return lax.rem(b + 2 * count, count)

    def place(b):
        if not folded:
            return around(b)
        b = around(b - 2)
        return 2 * b + (b // (count // 2)) * (2 * count - 1 - 4 * b)

    right, left = place(block + 1), place(block - 1)
    across = 1 - lax.axis_index("gy")
    barrier = pltpu.get_barrier_semaphore()
    greeted = [{"gx": around(me + k)} for k in (range(1, count) if folded else (1, -1))]
    for target in greeted + [{"gy": across}]:
        pl.semaphore_signal(barrier, inc=1, device_id=target, device_id_type=MESH)
    pl.semaphore_wait(barrier, len(greeted) + 1)
    leaving = []

    def route(number, source, landing, target, hop):
        remote = pltpu.make_async_remote_copy(
            src_ref=source, dst_ref=landing,
            send_sem=route_send.at[number], recv_sem=route_recv.at[number],
            device_id={"gx": target}, device_id_type=MESH,
        )
        here = pltpu.make_async_copy(source, landing, route_recv.at[number])
        if folded:
            pl.when(target == me)(here.start)
            pl.when(target != me)(remote.start)
            leaving.append(lambda: pl.when(target != me)(remote.wait_send))
            return remote.wait_recv
        if hop == 0:
            here.start()
            return here.wait
        remote.start()
        leaving.append(remote.wait_send)
        return remote.wait_recv

    got_state = route(0, state, q.at[0, :, mine], place(me), 0)
    got_high = route(1, state.at[:, pl.ds(0, HALO)], q.at[0, :, pl.ds(n + HALO, HALO)], place(me - 1), -1)
    got_low = route(2, state.at[:, pl.ds(n - HALO, HALO)], q.at[0, :, pl.ds(0, HALO)], place(me + 1), 1)
    got_closure = route(3, closure_in, closure, place(me), 0)
    got_state()
    late = []

    def three(number, sources, targets):
        made = []
        for k, (source, landing, target) in enumerate(
            zip(sources, targets, ({"gx": left}, {"gx": right}, {"gy": across}))
        ):
            made.append(
                pltpu.make_async_remote_copy(
                    src_ref=source, dst_ref=landing,
                    send_sem=send.at[number, k], recv_sem=recv.at[number, k],
                    device_id=target, device_id_type=MESH,
                )
            )
        return made

    pending = []

    def each(body, length=5):
        def step(i, carry):
            body(i)
            return carry
        lax.fori_loop(0, length, step, 0)

    def ring_y(s, c):
        return jnp.concatenate([q[s, c, mine], other[s, c]], axis=1)

    def forward(s):
        last = s == 2
        copies = three(
            s,
            (q.at[s, :, pl.ds(HALO, HALO)], q.at[s, :, pl.ds(n, HALO)], q.at[s, :, mine]),
            (q.at[s, :, pl.ds(n + HALO, HALO)], q.at[s, :, pl.ds(0, HALO)], other.at[s]),
        )
        if s == 0:
            copies = copies[2:]
        for copy in copies[::-1]:
            copy.start()
        pending.extend(copies)

        up, down = split_fluxes([q[s, c, mine] for c in range(5)], 2)
        for c in range(5):
            fz[0, c] = up[c]
            fz[1, c] = down[c]

        def along_z(c):
            face, coef = ring_weno(fz[0, c], 2, 1)
            face_low, coef_low = ring_weno(fz[1, c], 2, -1)
            for k in range(5):
                coef_z[s, c, 0, k] = coef[k]
                coef_z[s, c, 1, k] = coef_low[k]
            if not last:
                rate[c] = (shifted(face, -1, 2) - shifted(face_low, 1, 2)) + (face_low - face)
            own = q[s, c, mine]
            lap[s, c] = shifted(own, -1, 2) + shifted(own, 1, 2) - 6.0 * own

        for c in range(5):
            along_z(c)
        copies[-1].wait_recv()
        up, down = split_fluxes([ring_y(s, c) for c in range(5)], 1)
        for c in range(5):
            fy[0, c] = up[c]
            fy[1, c] = down[c]

        def along_y(c):
            face, coef = ring_weno(fy[0, c], 1, 1)
            face_low, coef_low = ring_weno(fy[1, c], 1, -1)
            for k in range(5):
                coef_y[s, c, 0, k] = coef[k]
                coef_y[s, c, 1, k] = coef_low[k]
            if not last:
                moved = shifted(face, -1, 1) - shifted(face_low, 1, 1)
                rate[c] += (moved + (face_low - face))[:, :8]
            both = ring_y(s, c)
            lap[s, c] += (shifted(both, -1, 1) + shifted(both, 1, 1))[:, :8]

        each(along_y)
        if s == 0:
            got_high()
            got_low()
            got_closure()
            late.append(route(4, cotangent, weight, place(me), 0))
        else:
            copies[0].wait_recv()
            copies[1].wait_recv()

        def flux_x(i):
            at = pl.ds(2 * i, 2)
            up, down = split_fluxes([q[s, c, at] for c in range(5)], 0)
            for c in range(5):
                fx[0, c, at] = up[c]
                fx[1, c, at] = down[c]

        each(flux_x, wide // 2)
        weight_base, weight_section = SECTION_WEIGHTS[s]

        def along_x(c):
            faces = [None] * (n + 1)
            for side, sign in ((0, 1), (1, -1)):
                f = [fx[side, c, i] for i in range(wide)]
                d = [f[i + 1] - f[i] for i in range(wide - 1)]
                bend = [None] + [d[i] - d[i - 1] for i in range(1, wide - 1)]
                m = [None] + [rough(b) for b in bend[1:]]
                for face in range(n + 1):
                    if sign > 0:
                        i = face + 2
                        value, coef = weno(
                            f[i], d[i - 1], d[i], bend[i - 1], bend[i], bend[i + 1],
                            m[i - 1], m[i], m[i + 1], 1)
                    else:
                        i = face + 3
                        value, coef = weno(
                            f[i], d[i], d[i - 1], bend[i + 1], bend[i], bend[i - 1],
                            m[i + 1], m[i], m[i - 1], -1)
                    faces[face] = plus(faces[face], value)
                    for k in range(5):
                        coef_x[s, c, side, k, face] = coef[k]
            on = jnp.where(c > 0, 1.0, 0.0)
            for x in range(n):
                i = x + HALO
                whole = lap[s, c, x] + q[s, c, i - 1] + q[s, c, i + 1]
                whole = whole * on
                lap[s, c, x] = whole
                if not last:
                    speed = rate[c, x] + (faces[x] - faces[x + 1]) + closure[x] * whole
                    q[s + 1, c, i] = (
                        weight_base * q[0, c, i] + weight_section * (q[s, c, i] + TIME_STEP * speed)
                    )

        each(along_x)

    def backward(s):
        weight_base, weight_section = SECTION_WEIGHTS[s]

        def along_x(c):
            on = jnp.where(c > 0, 1.0, 0.0)
            lams = []
            for x in range(n):
                here = weight[c, x]
                if weight_base:
                    total[c, x] += weight_base * here
                lams.append((TIME_STEP * weight_section) * here)
                lam[c, x] = lams[x]
                gin[c, x] = weight_section * here
            mus = [lams[0]] + [lams[x] - lams[x - 1] for x in range(1, n)] + [-lams[n - 1]]
            for side, sign in ((0, 1), (1, -1)):
                value = [None] * wide
                for face in range(n + 1):
                    i = face + 2 if sign > 0 else face + 3
                    for k in range(5):
                        at = i + sign * (k - 2)
                        value[at] = plus(value[at], coef_x[s, c, side, k, face] * mus[face])
                for i in range(wide):
                    fx[side, c, i] = jnp.zeros_like(mus[0]) if value[i] is None else value[i]
            kappa = [on * closure[x] * lams[x] for x in range(n)]
            for i in range(wide):
                x = i - HALO
                term = None
                if 0 <= x - 1 < n:
                    term = plus(term, kappa[x - 1])
                if 0 <= x + 1 < n:
                    term = plus(term, kappa[x + 1])
                if 0 <= x < n:
                    term = plus(term, -6.0 * kappa[x])
                gx[s, c, i] = jnp.zeros_like(mus[0]) if term is None else term

        each(along_x)

        def pull_x(i):
            at = pl.ds(2 * i, 2)
            grad = split_fluxes_back(
                [q[s, c, at] for c in range(5)],
                [fx[0, c, at] for c in range(5)],
                [fx[1, c, at] for c in range(5)], 0)
            for c in range(5):
                gx[s, c, at] += grad[c]

        each(pull_x, wide // 2)
        copies = three(
            HALO + s,
            (gx.at[s, :, pl.ds(0, HALO)], gx.at[s, :, pl.ds(n + HALO, HALO)], go.at[s]),
            (rx_high.at[s], rx_low.at[s], ro.at[s]),
        )
        if s == 0:
            copies = copies[2:]
            arrivals.append(route(
                5, gx.at[s, :, pl.ds(0, HALO)], rx_high.at[s], around(block - 1), -1))
            arrivals.append(route(
                6, gx.at[s, :, pl.ds(n + HALO, HALO)], rx_low.at[s], around(block + 1), 1))
        else:
            copies[0].start()
            copies[1].start()

        def along_y(c):
            on = jnp.where(c > 0, 1.0, 0.0)
            own = lam[c]
            ring = jnp.concatenate([own, jnp.zeros_like(own)], axis=1)
            mu = shifted(ring, 1, 1) - ring
            nu = ring - shifted(ring, -1, 1)
            fy[0, c] = ring_weno_back(mu, [coef_y[s, c, 0, k] for k in range(5)], 1, 1)
            fy[1, c] = ring_weno_back(nu, [coef_y[s, c, 1, k] for k in range(5)], 1, -1)
            kappa = own * closure[...] * on
            ring = jnp.concatenate([kappa, jnp.zeros_like(own)], axis=1)
            both = shifted(ring, 1, 1) + shifted(ring, -1, 1)
            gin[c] += both[:, :8] + shifted(kappa, 1, 2) + shifted(kappa, -1, 2)
            go[s, c] = both[:, 8:]

        each(along_y)

        def pull_y(x):
            grad = split_fluxes_back(
                [jnp.concatenate([q[s, c, x + HALO], other[s, c, x]], axis=0) for c in range(5)],
                [fy[0, c, x] for c in range(5)],
                [fy[1, c, x] for c in range(5)], 1)
            for c in range(5):
                gin[c, x] += grad[c][:8]
                go[s, c, x] += grad[c][8:]

        each(pull_y, n)
        copies[-1].start()
        pending.extend(copies)

        def along_z(c):
            own = lam[c]
            mu = shifted(own, 1, 2) - own
            nu = own - shifted(own, -1, 2)
            fz[0, c] = ring_weno_back(mu, [coef_z[s, c, 0, k] for k in range(5)], 2, 1)
            fz[1, c] = ring_weno_back(nu, [coef_z[s, c, 1, k] for k in range(5)], 2, -1)

        for c in range(5):
            along_z(c)

        def pull_z(i):
            at = pl.ds(2 * i, 2)
            inner = pl.ds(2 * i + HALO, 2)
            grad = split_fluxes_back(
                [q[s, c, inner] for c in range(5)],
                [fz[0, c, at] for c in range(5)],
                [fz[1, c, at] for c in range(5)], 2)
            for c in range(5):
                gin[c, at] += grad[c] + gx[s, c, inner]

        each(pull_z, n // 2)
        share = lam[1] * lap[s, 1]
        for c in range(2, 5):
            share = share + lam[c] * lap[s, c]
        grad_closure[...] = share if s == 2 else grad_closure[...] + share
        if s == 0:
            arrivals.append(route(7, grad_closure, home_closure, block, 0))
        for copy in copies:
            copy.wait_recv()

        def gather(c):
            if s == 0:
                gin[c] = gin[c] + ro[s, c] + total[c]
                return
            weight[c] = gin[c] + ro[s, c]
            weight[c, pl.ds(n - HALO, HALO)] += rx_high[s, c]
            weight[c, pl.ds(0, HALO)] += rx_low[s, c]

        each(gather)
        if s == 0:
            arrivals.append(route(8, gin, home, block, 0))

    arrivals = []
    for s in range(3):
        forward(s)
    late[0]()
    total[...] = jnp.zeros_like(total)
    for s in (2, 1, 0):
        backward(s)
    for arrived in arrivals:
        arrived()
    out_closure[...] = home_closure[...]

    def finish(c):
        out_state[c] = home[c]
        out_state[c, pl.ds(n - HALO, HALO)] += rx_high[0, c]
        out_state[c, pl.ds(0, HALO)] += rx_low[0, c]

    each(finish)
    for wait in leaving:
        wait()
    for copy in pending:
        copy.wait_send()


def local(state, closure, cotangent):
    _, n, rows, lanes = state.shape
    f32 = jnp.float32
    wide = n + 2 * HALO
    plane = (rows, lanes)

    def vmem(*shape):
        return pltpu.VMEM(shape + plane, f32)

    def tall(*shape):
        return pltpu.VMEM(shape + (2 * rows, lanes), f32)

    return pl.pallas_call(
        functools.partial(kernel, n),
        out_shape=(
            jax.ShapeDtypeStruct(state.shape, f32),
            jax.ShapeDtypeStruct(closure.shape, f32),
        ),
        in_specs=[pl.BlockSpec(memory_space=pl.ANY)] * 3,
        out_specs=(pl.BlockSpec(memory_space=pltpu.VMEM),) * 2,
        scratch_shapes=[
            vmem(n),
            vmem(3, 5, wide), vmem(3, 5, n),
            vmem(3, 5, 2, 5, n + 1), tall(3, 5, 2, 5, n), vmem(3, 5, 2, 5, n),
            vmem(3, 5, n), vmem(2, 5, wide), tall(2, 5, n), vmem(2, 5, n), vmem(5, n),
            vmem(5, n), vmem(5, n), vmem(5, n),
            vmem(3, 5, wide), vmem(3, 5, n), vmem(5, n),
            vmem(3, 5, HALO), vmem(3, 5, HALO), vmem(3, 5, n),
            pltpu.SemaphoreType.DMA((6, 3)), pltpu.SemaphoreType.DMA((6, 3)),
            vmem(5, n), vmem(n), vmem(n),
            pltpu.SemaphoreType.DMA((9,)), pltpu.SemaphoreType.DMA((9,)),
        ],
        compiler_params=pltpu.CompilerParams(
            collective_id=0, has_side_effects=True, vmem_limit_bytes=56 * 1024 * 1024
        ),
    )(state, closure, cotangent)


def solution(mesh):
    placed = (
        P("groups", "gx", "gy", None),
        P(("groups", "gx"), "gy", None),
        P("groups", "gx", "gy", None),
    )
    return jax.shard_map(
        local,
        mesh=mesh,
        in_specs=placed,
        out_specs=(P("groups", "gx", "gy", None), P(("groups", "gx"), "gy", None)),
        check_vma=False,
    )
```

```python
import functools
import jax
import jax.numpy as jnp
from jax import lax
from jax.experimental import pallas as pl
from jax.experimental.pallas import tpu as pltpu
from jax.sharding import PartitionSpec as P

WENO_EPS = 1e-06
TIME_STEP = 0.06
SECTION_WEIGHTS = ((0.0, 1.0), (0.75, 0.25), (1.0 / 3.0, 2.0 / 3.0))
HALO = 3
MESH = pl.DeviceIdType.MESH


def inverse_of(value):
    return 1.0 / value


def shifted(value, steps, axis):
    return pltpu.roll(value, (-steps) % value.shape[axis], axis)


def cell_terms(q, direction):
    inverse = inverse_of(q[0])
    squares = q[1] * q[1] + q[2] * q[2] + q[3] * q[3]
    pressure = 0.4 * (q[4] - 0.5 * squares * inverse)
    speed = q[1 + direction] * inverse
    inside = speed * speed + 1.4 * pressure * inverse
    root = lax.rsqrt(inside)
    return inverse, squares, pressure, speed, 1.5 * inside * root, root


def split_fluxes(q, direction):
    _, _, pressure, speed, wave, _ = cell_terms(q, direction)
    flux = [q[1 + direction], q[1] * speed, q[2] * speed, q[3] * speed, (q[4] + pressure) * speed]
    flux[1 + direction] = flux[1 + direction] + pressure
    half = 0.5 * wave
    up, down = [], []
    for c in range(5):
        centre, spread = 0.5 * flux[c], half * q[c]
        up.append(centre + spread)
        down.append(centre - spread)
    return up, down


def split_fluxes_back(q, up, down, direction):
    inverse, squares, pressure, speed, wave, root = cell_terms(q, direction)
    flux = [0.5 * (up[c] + down[c]) for c in range(5)]
    diff = [0.5 * (up[c] - down[c]) for c in range(5)]
    grad = [wave * diff[c] for c in range(5)]
    wave_bar = diff[0] * q[0] + diff[1] * q[1] + diff[2] * q[2] + diff[3] * q[3] + diff[4] * q[4]
    wave_bar = (1.5 * wave_bar) * root
    lift = flux[4] * speed
    ratio_bar = 0.7 * wave_bar
    speed_bar = (
        flux[1] * q[1] + flux[2] * q[2] + flux[3] * q[3]
        + flux[4] * (q[4] + pressure) + wave_bar * speed
    )
    pressure_bar = flux[1 + direction] + lift + ratio_bar * inverse
    inverse_bar = ratio_bar * pressure + speed_bar * q[1 + direction] - (0.2 * pressure_bar) * squares
    slope = 0.4 * pressure_bar
    pull = slope * inverse
    for k in range(1, 4):
        grad[k] = grad[k] + flux[k] * speed - pull * q[k]
    grad[1 + direction] = grad[1 + direction] + flux[0] + speed_bar * inverse
    grad[4] = grad[4] + lift + slope
    grad[0] = grad[0] - inverse_bar * inverse * inverse
    return grad


def rough(bend):
    return WENO_EPS + (13.0 / 12.0) * bend * bend


def weno(centre, d1, d2, s0, s1, s2, m0, m1, m2, sign):
    h0, h1, h2 = 0.5 * s0, 0.5 * s1, 0.5 * s2
    if sign > 0:
        t0, t1, t2 = h0 + d1, h1 + d1, h2 - d2
        base = centre + 0.5 * d1
    else:
        t0, t1, t2 = h0 - d1, h1 - d1, h2 + d2
        base = centre - 0.5 * d1
    r0, r1, r2 = inverse_of(m0 + t0 * t0), inverse_of(m1 + t1 * t1), inverse_of(m2 + t2 * t2)
    w0, w1, w2 = r0 * r0, 6.0 * (r1 * r1), 3.0 * (r2 * r2)
    scale = inverse_of(w0 + w1 + w2)
    w0, w1, w2 = w0 * scale, w1 * scale, w2 * scale
    third, sixth = 1.0 / 3.0, 1.0 / 6.0
    e0, e1, e2 = third * s0, third * s1, h1 - sixth * s2
    mean = w0 * e0 + w1 * e1 + w2 * e2
    c0, c1, c2 = w0 * r0 * (mean - e0), w1 * r1 * (mean - e1), w2 * r2 * (mean - e2)
    k = 13.0 / 3.0
    p0, p1, p2 = 2.0 * (c0 * t0), 2.0 * (c1 * t1), 2.0 * (c2 * t2)
    a0 = third * w0 + k * (c0 * s0) + p0
    a1 = third * w1 + 0.5 * w2 + k * (c1 * s1) + p1
    a2 = k * (c2 * s2) - sixth * w2 + p2
    j1 = a1 - 2.0 * a0 - (0.5 + 2.0 * (p0 + p1))
    j3 = a1 - 2.0 * (a2 + p2)
    j2 = 1.0 - (a0 + a2) - (j1 + j3)
    return base + mean, (a0, j1, j2, j3, a2)


def weno_of(v0, v1, v2, v3, v4):
    d0, d1, d2, d3 = v1 - v0, v2 - v1, v3 - v2, v4 - v3
    s0, s1, s2 = d1 - d0, d2 - d1, d3 - d2
    return weno(v2, d1, d2, s0, s1, s2, rough(s0), rough(s1), rough(s2), 1)


def ring_weno(f, axis, sign):
    v = [shifted(f, k, axis) if k else f for k in (-2, -1, 0, 1, 2)]
    return weno_of(*v[::sign])


def ring_weno_back(mu, coef, axis, sign):
    total = coef[2] * mu
    for k in (0, 1, 3, 4):
        total = total + shifted(coef[k] * mu, sign * (2 - k), axis)
    return total


def plus(total, term):
    return term if total is None else total + term


def kernel(
    n, state, closure_in, cotangent, out_state, out_closure, closure,
    q, other, coef_x, coef_y, coef_z, lap, fx, fy, fz, rate,
    lam, weight, total, gx, go, gin, rx_low, rx_high, ro, send, recv,
    home, home_closure, grad_closure, route_send, route_recv,
):
    wide = n + 2 * HALO
    mine = pl.ds(HALO, n)
    count = lax.axis_size("gx")
    me = lax.axis_index("gx")
    folded = count == 8
    if folded:
        block = lax.rem(me // 2 + (me % 2) * (count - 1 - 2 * (me // 2)) + 2, count)
    else:
        block = me

    def around(b):
        return lax.rem(b + 2 * count, count)

    def place(b):
        if not folded:
            return around(b)
        b = around(b - 2)
        return 2 * b + (b // (count // 2)) * (2 * count - 1 - 4 * b)

    right, left = place(block + 1), place(block - 1)
    across = 1 - lax.axis_index("gy")
    barrier = pltpu.get_barrier_semaphore()
    greeted = [{"gx": around(me + k)} for k in (range(1, count) if folded else (1, -1))]
    for target in greeted + [{"gy": across}]:
        pl.semaphore_signal(barrier, inc=1, device_id=target, device_id_type=MESH)
    pl.semaphore_wait(barrier, len(greeted) + 1)
    leaving = []

    def route(number, source, landing, target, hop):
        remote = pltpu.make_async_remote_copy(
            src_ref=source, dst_ref=landing,
            send_sem=route_send.at[number], recv_sem=route_recv.at[number],
            device_id={"gx": target}, device_id_type=MESH,
        )
        here = pltpu.make_async_copy(source, landing, route_recv.at[number])
        if folded:
            pl.when(target == me)(here.start)
            pl.when(target != me)(remote.start)
            leaving.append(lambda: pl.when(target != me)(remote.wait_send))
            return remote.wait_recv
        if hop == 0:
            here.start()
            return here.wait
        remote.start()
        leaving.append(remote.wait_send)
        return remote.wait_recv

    got_state = route(0, state, q.at[0, :, mine], place(me), 0)
    got_high = route(1, state.at[:, pl.ds(0, HALO)], q.at[0, :, pl.ds(n + HALO, HALO)], place(me - 1), -1)
    got_low = route(2, state.at[:, pl.ds(n - HALO, HALO)], q.at[0, :, pl.ds(0, HALO)], place(me + 1), 1)
    got_closure = route(3, closure_in, closure, place(me), 0)
    got_state()
    late = []

    def three(number, sources, targets):
        made = []
        for k, (source, landing, target) in enumerate(
            zip(sources, targets, ({"gx": left}, {"gx": right}, {"gy": across}))
        ):
            made.append(
                pltpu.make_async_remote_copy(
                    src_ref=source, dst_ref=landing,
                    send_sem=send.at[number, k], recv_sem=recv.at[number, k],
                    device_id=target, device_id_type=MESH,
                )
            )
        return made

    pending = []
    deferred = []

    def each(body, length=5):
        def step(i, carry):
            body(i)
            return carry
        lax.fori_loop(0, length, step, 0)

    def ring_y(s, c):
        return jnp.concatenate([q[s, c, mine], other[s, c]], axis=1)

    def forward(s):
        last = s == 2
        copies = three(
            s,
            (q.at[s, :, pl.ds(HALO, HALO)], q.at[s, :, pl.ds(n, HALO)], q.at[s, :, mine]),
            (q.at[s, :, pl.ds(n + HALO, HALO)], q.at[s, :, pl.ds(0, HALO)], other.at[s]),
        )
        if s == 0:
            copies = copies[2:]
        for copy in copies[::-1]:
            copy.start()
        pending.extend(copies)
        while deferred:
            each(deferred.pop())

        up, down = split_fluxes([q[s, c, mine] for c in range(5)], 2)
        for c in range(5):
            fz[0, c] = up[c]
            fz[1, c] = down[c]

        def along_z(c):
            face, coef = ring_weno(fz[0, c], 2, 1)
            face_low, coef_low = ring_weno(fz[1, c], 2, -1)
            for k in range(5):
                coef_z[s, c, 0, k] = coef[k]
                coef_z[s, c, 1, k] = coef_low[k]
            if not last:
                rate[c] = (shifted(face, -1, 2) - shifted(face_low, 1, 2)) + (face_low - face)
            own = q[s, c, mine]
            lap[s, c] = shifted(own, -1, 2) + shifted(own, 1, 2) - 6.0 * own

        for c in range(5):
            along_z(c)
        copies[-1].wait_recv()
        up, down = split_fluxes([ring_y(s, c) for c in range(5)], 1)
        for c in range(5):
            fy[0, c] = up[c]
            fy[1, c] = down[c]

        def along_y(c):
            face, coef = ring_weno(fy[0, c], 1, 1)
            face_low, coef_low = ring_weno(fy[1, c], 1, -1)
            for k in range(5):
                coef_y[s, c, 0, k] = coef[k]
                coef_y[s, c, 1, k] = coef_low[k]
            if not last:
                moved = shifted(face, -1, 1) - shifted(face_low, 1, 1)
                rate[c] += (moved + (face_low - face))[:, :8]
            both = ring_y(s, c)
            lap[s, c] += (shifted(both, -1, 1) + shifted(both, 1, 1))[:, :8]

        each(along_y)
        if s == 0:
            got_high()
            got_low()
            got_closure()
            late.append(route(4, cotangent, weight, place(me), 0))
        else:
            copies[0].wait_recv()
            copies[1].wait_recv()

        def flux_x(i):
            at = pl.ds(2 * i, 2)
            up, down = split_fluxes([q[s, c, at] for c in range(5)], 0)
            for c in range(5):
                fx[0, c, at] = up[c]
                fx[1, c, at] = down[c]

        each(flux_x, wide // 2)
        weight_base, weight_section = SECTION_WEIGHTS[s]

        def coefs_x(c):
            along_x(c, False, True)

        def values_x(c):
            along_x(c, True, last)

        def along_x(c, update, store):
            faces = [None] * (n + 1)
            for side, sign in ((0, 1), (1, -1)):
                f = [fx[side, c, i] for i in range(wide)]
                d = [f[i + 1] - f[i] for i in range(wide - 1)]
                bend = [None] + [d[i] - d[i - 1] for i in range(1, wide - 1)]
                m = [None] + [rough(b) for b in bend[1:]]
                for face in range(n + 1):
                    if sign > 0:
                        i = face + 2
                        value, coef = weno(
                            f[i], d[i - 1], d[i], bend[i - 1], bend[i], bend[i + 1],
                            m[i - 1], m[i], m[i + 1], 1)
                    else:
                        i = face + 3
                        value, coef = weno(
                            f[i], d[i], d[i - 1], bend[i + 1], bend[i], bend[i - 1],
                            m[i + 1], m[i], m[i - 1], -1)
                    faces[face] = plus(faces[face], value)
                    for k in range(5):
                        if store:
                            coef_x[s, c, side, k, face] = coef[k]
            if not update:
                return
            on = jnp.where(c > 0, 1.0, 0.0)
            for x in range(n):
                i = x + HALO
                whole = lap[s, c, x] + q[s, c, i - 1] + q[s, c, i + 1]
                whole = whole * on
                lap[s, c, x] = whole
                if not last:
                    speed = rate[c, x] + (faces[x] - faces[x + 1]) + closure[x] * whole
                    q[s + 1, c, i] = (
                        weight_base * q[0, c, i] + weight_section * (q[s, c, i] + TIME_STEP * speed)
                    )

        each(values_x)
        if not last:
            deferred.append(coefs_x)

    def backward(s):
        weight_base, weight_section = SECTION_WEIGHTS[s]

        def along_x(c):
            on = jnp.where(c > 0, 1.0, 0.0)
            lams = []
            for x in range(n):
                here = weight[c, x]
                if weight_base:
                    total[c, x] += weight_base * here
                lams.append((TIME_STEP * weight_section) * here)
                lam[c, x] = lams[x]
                gin[c, x] = weight_section * here
            mus = [lams[0]] + [lams[x] - lams[x - 1] for x in range(1, n)] + [-lams[n - 1]]
            for side, sign in ((0, 1), (1, -1)):
                value = [None] * wide
                for face in range(n + 1):
                    i = face + 2 if sign > 0 else face + 3
                    for k in range(5):
                        at = i + sign * (k - 2)
                        value[at] = plus(value[at], coef_x[s, c, side, k, face] * mus[face])
                for i in range(wide):
                    fx[side, c, i] = jnp.zeros_like(mus[0]) if value[i] is None else value[i]
            kappa = [on * closure[x] * lams[x] for x in range(n)]
            for i in range(wide):
                x = i - HALO
                term = None
                if 0 <= x - 1 < n:
                    term = plus(term, kappa[x - 1])
                if 0 <= x + 1 < n:
                    term = plus(term, kappa[x + 1])
                if 0 <= x < n:
                    term = plus(term, -6.0 * kappa[x])
                gx[s, c, i] = jnp.zeros_like(mus[0]) if term is None else term

        each(along_x)

        def pull_x(start, width):
            at = pl.ds(start, width)
            grad = split_fluxes_back(
                [q[s, c, at] for c in range(5)],
                [fx[0, c, at] for c in range(5)],
                [fx[1, c, at] for c in range(5)], 0)
            for c in range(5):
                gx[s, c, at] += grad[c]

        pull_x(0, HALO)
        pull_x(n + HALO, HALO)
        copies = three(
            HALO + s,
            (gx.at[s, :, pl.ds(0, HALO)], gx.at[s, :, pl.ds(n + HALO, HALO)], go.at[s]),
            (rx_high.at[s], rx_low.at[s], ro.at[s]),
        )
        if s == 0:
            copies = copies[2:]
            arrivals.append(route(
                5, gx.at[s, :, pl.ds(0, HALO)], rx_high.at[s], around(block - 1), -1))
            arrivals.append(route(
                6, gx.at[s, :, pl.ds(n + HALO, HALO)], rx_low.at[s], around(block + 1), 1))
        else:
            copies[0].start()
            copies[1].start()
        pull_x(HALO, n)

        def along_y(c):
            on = jnp.where(c > 0, 1.0, 0.0)
            own = lam[c]
            ring = jnp.concatenate([own, jnp.zeros_like(own)], axis=1)
            mu = shifted(ring, 1, 1) - ring
            nu = ring - shifted(ring, -1, 1)
            fy[0, c] = ring_weno_back(mu, [coef_y[s, c, 0, k] for k in range(5)], 1, 1)
            fy[1, c] = ring_weno_back(nu, [coef_y[s, c, 1, k] for k in range(5)], 1, -1)
            kappa = own * closure[...] * on
            ring = jnp.concatenate([kappa, jnp.zeros_like(own)], axis=1)
            both = shifted(ring, 1, 1) + shifted(ring, -1, 1)
            gin[c] += both[:, :8] + shifted(kappa, 1, 2) + shifted(kappa, -1, 2)
            go[s, c] = both[:, 8:]

        each(along_y)

        def pull_y(x):
            grad = split_fluxes_back(
                [jnp.concatenate([q[s, c, x + HALO], other[s, c, x]], axis=0) for c in range(5)],
                [fy[0, c, x] for c in range(5)],
                [fy[1, c, x] for c in range(5)], 1)
            for c in range(5):
                gin[c, x] += grad[c][:8]
                go[s, c, x] += grad[c][8:]

        each(pull_y, n)
        copies[-1].start()
        pending.extend(copies)

        def along_z(c):
            own = lam[c]
            mu = shifted(own, 1, 2) - own
            nu = own - shifted(own, -1, 2)
            fz[0, c] = ring_weno_back(mu, [coef_z[s, c, 0, k] for k in range(5)], 2, 1)
            fz[1, c] = ring_weno_back(nu, [coef_z[s, c, 1, k] for k in range(5)], 2, -1)

        for c in range(5):
            along_z(c)

        def pull_z(i):
            at = pl.ds(2 * i, 2)
            inner = pl.ds(2 * i + HALO, 2)
            grad = split_fluxes_back(
                [q[s, c, inner] for c in range(5)],
                [fz[0, c, at] for c in range(5)],
                [fz[1, c, at] for c in range(5)], 2)
            for c in range(5):
                gin[c, at] += grad[c] + gx[s, c, inner]

        each(pull_z, n // 2)
        share = lam[1] * lap[s, 1]
        for c in range(2, 5):
            share = share + lam[c] * lap[s, c]
        grad_closure[...] = share if s == 2 else grad_closure[...] + share
        if s == 0:
            arrivals.append(route(7, grad_closure, home_closure, block, 0))
        for copy in copies:
            copy.wait_recv()

        def gather(c):
            if s == 0:
                gin[c] = gin[c] + ro[s, c] + total[c]
                return
            weight[c] = gin[c] + ro[s, c]
            weight[c, pl.ds(n - HALO, HALO)] += rx_high[s, c]
            weight[c, pl.ds(0, HALO)] += rx_low[s, c]

        each(gather)
        if s == 0:
            arrivals.append(route(8, gin, home, block, 0))

    arrivals = []
    for s in range(3):
        forward(s)
    late[0]()
    total[...] = jnp.zeros_like(total)
    for s in (2, 1, 0):
        backward(s)
    for arrived in arrivals:
        arrived()
    out_closure[...] = home_closure[...]

    def finish(c):
        out_state[c] = home[c]
        out_state[c, pl.ds(n - HALO, HALO)] += rx_high[0, c]
        out_state[c, pl.ds(0, HALO)] += rx_low[0, c]

    each(finish)
    for wait in leaving:
        wait()
    for copy in pending:
        copy.wait_send()


def local(state, closure, cotangent):
    _, n, rows, lanes = state.shape
    f32 = jnp.float32
    wide = n + 2 * HALO
    plane = (rows, lanes)

    def vmem(*shape):
        return pltpu.VMEM(shape + plane, f32)

    def tall(*shape):
        return pltpu.VMEM(shape + (2 * rows, lanes), f32)

    return pl.pallas_call(
        functools.partial(kernel, n),
        out_shape=(
            jax.ShapeDtypeStruct(state.shape, f32),
            jax.ShapeDtypeStruct(closure.shape, f32),
        ),
        in_specs=[pl.BlockSpec(memory_space=pl.ANY)] * 3,
        out_specs=(pl.BlockSpec(memory_space=pltpu.VMEM),) * 2,
        scratch_shapes=[
            vmem(n),
            vmem(3, 5, wide), vmem(3, 5, n),
            vmem(3, 5, 2, 5, n + 1), tall(3, 5, 2, 5, n), vmem(3, 5, 2, 5, n),
            vmem(3, 5, n), vmem(2, 5, wide), tall(2, 5, n), vmem(2, 5, n), vmem(5, n),
            vmem(5, n), vmem(5, n), vmem(5, n),
            vmem(3, 5, wide), vmem(3, 5, n), vmem(5, n),
            vmem(3, 5, HALO), vmem(3, 5, HALO), vmem(3, 5, n),
            pltpu.SemaphoreType.DMA((6, 3)), pltpu.SemaphoreType.DMA((6, 3)),
            vmem(5, n), vmem(n), vmem(n),
            pltpu.SemaphoreType.DMA((9,)), pltpu.SemaphoreType.DMA((9,)),
        ],
        compiler_params=pltpu.CompilerParams(
            collective_id=0, has_side_effects=True, vmem_limit_bytes=56 * 1024 * 1024
        ),
    )(state, closure, cotangent)


def solution(mesh):
    placed = (
        P("groups", "gx", "gy", None),
        P(("groups", "gx"), "gy", None),
        P("groups", "gx", "gy", None),
    )
    return jax.shard_map(
        local,
        mesh=mesh,
        in_specs=placed,
        out_specs=(P("groups", "gx", "gy", None), P(("groups", "gx"), "gy", None)),
        check_vma=False,
    )
```
